512 devices in a mesh: head: 8 (over x, z_lo), blk: 64 (over y, z_hi, core).
Axes of the slice: x: 4, y: 8, z: 8 (z_hi: 4, z_lo: 2; z = z_hi * 2 + z_lo), core: 2. Of those that a mesh axis runs over, the one named last changes fastest.
Arguments:
- queries: bfloat16 [65536, 2048], P(('blk', 'head')), may hold values from -4 to 4
- keys: bfloat16 [65536, 2048], P(('blk', 'head')), may hold values from -4 to 4
- values: bfloat16 [65536, 2048], P(('blk', 'head')), may hold values from -6 to 6
- outputs: bfloat16 [65536, 2048], P(('blk', 'head')), may hold values from -6 to 6
- out_grad: bfloat16 [65536, 2048], P(('blk', 'head')), may hold values from -96 to 96
- log_sum: float32 [65536, 16], P(('blk', 'head')), may hold values from 7 to 9
Outputs:
- query_grad: bfloat16 [65536, 2048], P(('blk', 'head'))
- key_grad: bfloat16 [65536, 2048], P(('blk', 'head'))
- value_grad: bfloat16 [65536, 2048], P(('blk', 'head'))
The draws below stay inside these ranges and needn't reach their ends.
All inputs are finite; a program needn't handle non-finite values.
Results may differ from the reference program's by a relative error of at most 0.0053.
Values may be sent and summed in bfloat16 or wider, within the bound.
A program may use at most 64 MiB of HBM per device.

```python
import jax
import jax.numpy as jnp
from jax import lax

H = 16
HD = 128
REACH = 1
SPAN = 512
BLOCKS = 128
TOK = 65536
WIDTH = 2048


def block_levels(stream_key, shape, pieces, low, largest):
    factor_of = 1.0
    for axis_at, blocks in pieces:
        steps = jax.random.uniform(jax.random.fold_in(jax.random.fold_in(stream_key, 6), axis_at), (blocks,), jnp.float32, low / len(pieces), largest / len(pieces))
        factor_of = factor_of * jnp.repeat(jnp.exp(steps), shape[axis_at] // blocks).reshape((-1,) + (1,) * (len(shape) - 1 - axis_at))
    return factor_of


def centred(stream_key, extent, spread, reach, shards=(), dtype=jnp.bfloat16):
    values = jax.random.normal(stream_key, extent, jnp.float32) * spread
    if len(shards) > 0:
        values = block_levels(stream_key, extent, shards, -0.22, 0.18) * values
    return jnp.clip(values, min=-reach, max=reach).astype(dtype)


def setup_inputs(seed: int = 0) -> dict:
    arg_keys = jax.random.split(jax.random.key(seed), 7)
    queries = centred(arg_keys[0], (TOK, WIDTH), 1.0, 4.0, ((0, 512),))
    keys = centred(arg_keys[1], (TOK, WIDTH), 1.0, 4.0, ((0, 512),))
    values = centred(arg_keys[2], (TOK, WIDTH), 1.0, 6.0, ((0, 512),))
    outputs = centred(arg_keys[3], (TOK, WIDTH), 1.0, 6.0, ((0, 512),))
    out_grad = centred(arg_keys[4], (TOK, WIDTH), 16.0, 96.0, ((0, 512),))
    log_sum = jnp.clip(7.0 + 2.0 * jax.random.uniform(arg_keys[5], (TOK, H), jnp.float32) ** block_levels(arg_keys[5], (TOK, H), ((0, 512),), -0.2, 0.2), 7.0, 9.0)
    return dict(queries=queries, keys=keys, values=values, outputs=outputs, out_grad=out_grad, log_sum=log_sum)


def per_head(packed):
    query_h, key_h, value_h, output_h, grad_h, lse_h = packed
    softmax_scale = HD ** -0.5

    def blocks(array):
        return array.reshape(BLOCKS, SPAN, HD).astype(jnp.float32)

    query_block = blocks(query_h)
    key_b = blocks(key_h)
    value_b = blocks(value_h)
    gradient_block = blocks(grad_h)
    output_b = blocks(output_h)
    lse_b = lse_h.reshape(BLOCKS, SPAN)
    delta = jnp.sum(gradient_block * output_b, axis=2)
    summed_query = jnp.zeros((BLOCKS, SPAN, HD), jnp.float32)
    key_sum = jnp.zeros((BLOCKS, SPAN, HD), jnp.float32)
    value_sum = jnp.zeros((BLOCKS, SPAN, HD), jnp.float32)
    for offset in range(-REACH, REACH + 1):
        neighbor_keys = jnp.roll(key_b, -offset, axis=0)
        neighbor_values = jnp.roll(value_b, -offset, axis=0)
        score_matrix = jnp.einsum("nsl,njl->nsj", query_block, neighbor_keys) * softmax_scale
        attend = jnp.exp(score_matrix - lse_b[:, :, None])
        weights_reduced = lax.optimization_barrier(attend.astype(jnp.bfloat16)).astype(jnp.float32)
        value_portion = jnp.einsum("chp,chu->cpu", weights_reduced, gradient_block)
        weights_gradient = jnp.einsum("nsl,njl->nsj", gradient_block, neighbor_values)
        logits_gradient = lax.optimization_barrier((attend * (weights_gradient - delta[:, :, None])).astype(jnp.bfloat16)).astype(jnp.float32)
        summed_query = summed_query + jnp.einsum("icv,iva->ica", logits_gradient, neighbor_keys) * softmax_scale
        key_portion = jnp.einsum("chp,chu->cpu", logits_gradient, query_block) * softmax_scale
        key_sum = key_sum + jnp.roll(key_portion, offset, axis=0)
        value_sum = value_sum + jnp.roll(value_portion, offset, axis=0)

    def finish(array):
        return array.reshape(TOK, HD).astype(jnp.bfloat16)

    return finish(summed_query), finish(key_sum), finish(value_sum)


def reference(queries, keys, values, outputs, out_grad, log_sum):
    def split_heads(array):
        return jnp.transpose(array.reshape(TOK, H, HD), (1, 0, 2))

    def merge_heads(array):
        return jnp.transpose(array, (1, 0, 2)).reshape(TOK, H * HD)

    packed = (split_heads(queries), split_heads(keys), split_heads(values), split_heads(outputs), split_heads(out_grad), jnp.transpose(log_sum))
    query_all, key_all, value_all = lax.map(per_head, packed)
    return merge_heads(query_all), merge_heads(key_all), merge_heads(value_all)
```

```python
import math

import jax
import jax.numpy as jnp
from jax import lax
from jax.experimental import pallas as pl
from jax.experimental.pallas import tpu as pltpu
from jax.sharding import PartitionSpec as P

MESH = pl.DeviceIdType.MESH
HD = 128
SCALE = HD**-0.5
LOG2E = math.log2(math.e)
F32 = jnp.float32
BF16 = jnp.bfloat16
NX = 4
SLOTS = 2 * NX
BLOCKS = 4
ROWS = SLOTS * 128
HALF = 256


def nt(a, b, **kw):
    return lax.dot_general(a, b, (((1,), (1,)), ((), ())), preferred_element_type=F32, **kw)


def nn(a, b, **kw):
    return lax.dot_general(a, b, (((1,), (0,)), ((), ())), preferred_element_type=F32, **kw)


def tn(a, b):
    return lax.dot_general(a, b, (((0,), (0,)), ((), ())), preferred_element_type=F32)


def tile(k, v, q, g, lse, delta):
    p = jnp.exp2(nt(k, q) * (SCALE * LOG2E) - lse)
    ds = (p * (nt(v, g) - delta)).astype(BF16)
    dv = nn(p.astype(BF16), g)
    dk = nn(ds, q)
    dq = tn(ds, k)
    return dk, dv, dq


def kernel(
    groups,
    q_in, k_in, v_in, o_in, g_in, l_in,
    dq_res, dk_res, dv_res,
    qg, kv, kvp, eqg, st_all, st, est, g_v, o_v, l_v,
    dq_acc, dq_own, dk_acc, dv_acc,
    dq_oth, dq_got, dq_out, dk_out, dv_out, dqe_out, dqe_got, dkv_out, dkv_got,
    loc, r_qg, r_kv, r_b, r_k, r_c, r_st, r_dqe, r_dkv, r_d, r_out,
    s_a, s_b, s_k, s_c, s_st, s_st2, s_dqe, s_dkv, s_d, s_out,
):
    head = lax.axis_index("head")
    blk = lax.axis_index("blk")
    x = lax.div(head, 2)
    zl = lax.rem(head, 2)
    grp = lax.div(blk, 2)
    c = lax.rem(blk, 2)
    me_t = x * 2 + c
    me_s = c * NX + x
    my_b = lax.div(me_s, 2)
    eb = 3 * zl
    pb = 3 - eb
    partner = (x * 2 + (1 - zl), blk)
    near = (x * 2 + (1 - zl), lax.rem(grp + 2 * zl - 1 + groups, groups) * 2 + c)

    def at_t(t):
        return (lax.div(t, 2) * 2 + zl, grp * 2 + lax.rem(t, 2))

    def at_s(s):
        return (lax.rem(s, NX) * 2 + zl, grp * 2 + lax.div(s, NX))

    def rows(b):
        return pl.ds(pl.multiple_of(b * HALF, HALF), HALF)

    def run(s):
        return pl.ds(pl.multiple_of(s * 128, 128), 128)

    def cols(t, hl):
        return pl.ds(pl.multiple_of(t * 256 + hl * 128, 128), 128)

    def remote(src, dst, ssem, rsem, device):
        copy = pltpu.make_async_remote_copy(
            src_ref=src, dst_ref=dst, send_sem=ssem, recv_sem=rsem, device_id=device, device_id_type=MESH
        )
        copy.start()
        return copy

    def arrived(ref, sem):
        pltpu.make_async_copy(ref, ref, sem).wait()

    pending = []

    locals_ = [
        pltpu.make_async_copy(g_in, g_v, loc.at[0]),
        pltpu.make_async_copy(o_in, o_v, loc.at[1]),
        pltpu.make_async_copy(l_in, l_v, loc.at[2]),
    ]
    for copy in locals_:
        copy.start()

    barrier = pltpu.get_barrier_semaphore()
    for o in range(1, SLOTS):
        pl.semaphore_signal(
            barrier, inc=1, device_id=at_t(lax.rem(me_t + o, SLOTS)), device_id_type=MESH
        )
    for device in (partner, near):
        pl.semaphore_signal(barrier, inc=1, device_id=device, device_id_type=MESH)
    pl.semaphore_wait(barrier, SLOTS + 1)

    def spread(hl, which):
        arrays = ((q_in, qg.at[0, 0, hl], 0), (g_in, qg.at[0, 1, hl], 1)) if which == 0 else (
            (k_in, kv.at[0, hl], 2), (v_in, kv.at[1, hl], 3))
        rsem = r_qg.at[hl, my_b] if which == 0 else r_kv.at[hl]
        for src, dst, _ in arrays:
            pltpu.make_async_copy(src.at[:, cols(me_t, hl)], dst.at[run(me_s)], rsem).start()
        for o in range(1, SLOTS):
            t = lax.rem(me_t + o, SLOTS)
            for src, dst, n in arrays:
                remote(src.at[:, cols(t, hl)], dst.at[run(me_s)], s_a.at[n, hl], rsem, at_t(t))

    spread(0, 0)
    spread(0, 1)

    for copy in locals_:
        copy.wait()
    r = lax.broadcasted_iota(jnp.int32, (8 * SLOTS, SLOTS * 256), 0)
    col = lax.broadcasted_iota(jnp.int32, (8 * SLOTS, SLOTS * 256), 1)
    wanted = lax.shift_right_logical(r, 3) * 2 + lax.shift_right_logical(r & 7, 1)
    pick = jnp.where(
        (lax.shift_right_logical(col, 7) == wanted) & ((r & 1) == 1) & ((r & 7) < 4), 1.0, 0.0
    ).astype(F32)
    prod = g_v[...].astype(F32) * o_v[...].astype(F32)
    delta_rows = nt(pick, prod, precision=lax.Precision.HIGHEST)
    r2 = lax.broadcasted_iota(jnp.int32, (8 * SLOTS, 2 * SLOTS), 0)
    col2 = lax.broadcasted_iota(jnp.int32, (8 * SLOTS, 2 * SLOTS), 1)
    wanted2 = lax.shift_right_logical(r2, 3) * 2 + lax.shift_right_logical(r2 & 7, 1)
    pick2 = jnp.where((col2 == wanted2) & ((r2 & 1) == 0) & ((r2 & 7) < 4), 1.0, 0.0).astype(F32)
    lse_rows = nn(pick2, l_v[...], precision=lax.Precision.HIGHEST) * LOG2E
    st_all[...] = delta_rows + lse_rows
    mine = st_all.at[pl.ds(pl.multiple_of(me_t * 8, 8), 8)]
    pltpu.make_async_copy(mine, st.at[0, me_s], r_st.at[0]).start()
    for o in range(1, SLOTS):
        t = lax.rem(me_t + o, SLOTS)
        pending.append(remote(
            st_all.at[pl.ds(pl.multiple_of(t * 8, 8), 8)], st.at[0, me_s], s_st.at[o], r_st.at[0], at_t(t)
        ))

    dk_acc[...] = jnp.zeros_like(dk_acc)
    dv_acc[...] = jnp.zeros_like(dv_acc)

    order = [pb + i * (1 - 2 * lax.div(pb, 3)) for i in range(BLOCKS)]

    def forward(hl):
        for b in order:
            arrived(qg.at[0, :, hl, rows(b)], r_qg.at[hl, b])
            pending.append(remote(
                qg.at[0, :, hl, rows(b)], qg.at[1, :, hl, rows(b)], s_b.at[hl, b], r_b.at[hl, b], partner
            ))
        pending.append(remote(
            qg.at[0, :, hl, rows(eb)], eqg.at[hl, :, pl.ds(0, HALF)], s_c.at[hl, 0], r_c.at[hl], near
        ))

    def forward_kv(hl):
        arrived(kv.at[:, hl], r_kv.at[hl])
        pending.append(remote(kv.at[:, hl, rows(pb)], kvp.at[hl], s_k.at[hl], r_k.at[hl], partner))

    def forward_edge(hl):
        arrived(qg.at[1, :, hl, rows(eb)], r_b.at[hl, eb])
        pending.append(remote(
            qg.at[1, :, hl, rows(eb)], eqg.at[hl, :, pl.ds(HALF, HALF)], s_c.at[hl, 1], r_c.at[hl], near
        ))

    forward(0)
    spread(1, 0)
    arrived(st.at[0], r_st.at[0])
    pending.append(remote(st.at[0], st.at[1], s_st2.at[0], r_st.at[1], partner))
    forward_kv(0)
    spread(1, 1)
    arrived(st.at[1], r_st.at[1])
    pending.append(remote(st.at[:, pl.ds(2 * eb, 2)], est, s_st2.at[1], r_st.at[2], near))
    forward_edge(0)
    forward(1)
    arrived(est, r_st.at[2])

    def stat(ref, first, hl, n):
        place = 2 * hl + n
        return jnp.concatenate(
            [ref[p, first + j, place : place + 1, :] for p in range(2) for j in range(2)], axis=1
        )

    def edge(hl):
        arrived(kvp.at[hl], r_k.at[hl])
        arrived(eqg.at[hl], r_c.at[hl])
        q = eqg[hl, 0]
        g = eqg[hl, 1]
        lse = stat(est, 0, hl, 0)
        delta = stat(est, 0, hl, 1)
        dk, dv, dq = tile(kvp[hl, 0], kvp[hl, 1], q, g, lse, delta)
        dkv_out[hl, 0] = (dk * SCALE).astype(BF16)
        dkv_out[hl, 1] = dv.astype(BF16)
        pending.append(remote(dkv_out.at[hl], dkv_got.at[hl], s_dkv.at[hl], r_dkv.at[hl], partner))
        dk, dv, dq2 = tile(kv[0, hl, rows(eb)], kv[1, hl, rows(eb)], q, g, lse, delta)
        dqe_out[hl] = ((dq + dq2) * SCALE).astype(BF16)
        pending.append(remote(dqe_out.at[hl], dqe_got.at[hl], s_dqe.at[hl], r_dqe.at[hl], near))
        dk_acc[hl, rows(eb)] += dk
        dv_acc[hl, rows(eb)] += dv

    def give_back(buf, res, n, hl, b):
        for j in range(2):
            s = 2 * b + j
            src = buf.at[hl, run(s)]
            dst = res.at[:, cols(me_t, hl)]

            @pl.when(s == me_s)
            def _():
                pltpu.make_async_copy(src, dst, r_out.at[n]).start()

            @pl.when(s != me_s)
            def _():
                remote(src, dst, s_out.at[n], r_out.at[n], at_s(s))

    def finish_keys(hl, b, first):
        dk = dk_acc[hl, rows(b)] * SCALE
        dv = dv_acc[hl, rows(b)]
        if first:
            arrived(dkv_got.at[hl], r_dkv.at[hl])
            dk = dk + dkv_got[hl, 0].astype(F32)
            dv = dv + dkv_got[hl, 1].astype(F32)
        dk_out[hl, rows(b)] = dk.astype(BF16)
        dv_out[hl, rows(b)] = dv.astype(BF16)
        give_back(dk_out, dk_res, 1, hl, b)
        give_back(dv_out, dv_res, 2, hl, b)

    def finish_queries(hl, b):
        arrived(dq_got.at[hl, rows(b)], r_d.at[hl, b])
        dq_out[hl, rows(b)] = (dq_own[hl, rows(b)] + dq_got[hl, rows(b)].astype(F32)).astype(BF16)
        give_back(dq_out, dq_res, 0, hl, b)

    def main(hl, i):
        b = order[i]
        if i < BLOCKS - 1:
            arrived(qg.at[1, :, hl, rows(b)], r_b.at[hl, b])
        q = jnp.concatenate([qg[0, 0, hl, rows(b)], qg[1, 0, hl, rows(b)]], axis=0)
        g = jnp.concatenate([qg[0, 1, hl, rows(b)], qg[1, 1, hl, rows(b)]], axis=0)
        lse = stat(st, 2 * b, hl, 0)
        delta = stat(st, 2 * b, hl, 1)
        dq_acc[...] = jnp.zeros_like(dq_acc)

        def body(kb, carry):
            dk, dv, dq = tile(kv[0, hl, rows(kb)], kv[1, hl, rows(kb)], q, g, lse, delta)
            dk_acc[hl, rows(kb)] += dk
            dv_acc[hl, rows(kb)] += dv
            dq_acc[...] += dq
            return carry

        lax.fori_loop(jnp.maximum(b - 1, 0), jnp.minimum(b + 1, BLOCKS - 1) + 1, body, 0)
        own = dq_acc[pl.ds(0, HALF)] * SCALE
        other = dq_acc[pl.ds(HALF, HALF)] * SCALE
        if i == BLOCKS - 1:
            arrived(dqe_got.at[hl], r_dqe.at[hl])
            own = own + dqe_got[hl, pl.ds(0, HALF)].astype(F32)
            other = other + dqe_got[hl, pl.ds(HALF, HALF)].astype(F32)
        dq_oth[hl, rows(b)] = other.astype(BF16)
        pending.append(remote(
            dq_oth.at[hl, rows(b)], dq_got.at[hl, rows(b)], s_d.at[hl, b], r_d.at[hl, b], partner
        ))
        dq_own[hl, rows(b)] = own
        if i >= 1:
            finish_keys(hl, order[i - 1], i == 1)

    edge(0)
    forward_kv(1)
    forward_edge(1)
    for i in range(BLOCKS):
        main(0, i)
    finish_keys(0, order[BLOCKS - 1], False)
    edge(1)
    for i in reversed(range(BLOCKS)):
        finish_queries(0, order[i])
    for i in range(BLOCKS - 1):
        main(1, i)
    finish_queries(1, order[2])
    main(1, BLOCKS - 1)
    finish_keys(1, order[BLOCKS - 1], False)
    for i in (1, 3, 0):
        finish_queries(1, order[i])

    for copy in pending:
        copy.wait_send()
    for n in range(4):
        for hl in range(2):
            arrived(kv.at[0, 0, pl.ds(0, 7 * 128)], s_a.at[n, hl])
    for n, res in enumerate((dq_res, dk_res, dv_res)):
        arrived(dk_out.at[:, pl.ds(0, 7 * 128)], s_out.at[n])
        arrived(res, r_out.at[n])


def per_device(queries, keys, values, outputs, out_grad, log_sum):
    groups = lax.axis_size("blk") // 2
    tokens, width = queries.shape
    any_ = pl.BlockSpec(memory_space=pl.ANY)
    dma = pltpu.SemaphoreType.DMA
    result = jax.ShapeDtypeStruct((tokens, width), BF16)
    scratch = [
        pltpu.VMEM((2, 2, 2, ROWS, HD), BF16),
        pltpu.VMEM((2, 2, ROWS, HD), BF16),
        pltpu.VMEM((2, 2, HALF, HD), BF16),
        pltpu.VMEM((2, 2, 2 * HALF, HD), BF16),
        pltpu.VMEM((8 * SLOTS, 128), F32),
        pltpu.VMEM((2, SLOTS, 8, 128), F32),
        pltpu.VMEM((2, 2, 8, 128), F32),
        pltpu.VMEM((tokens, width), BF16),
        pltpu.VMEM((tokens, width), BF16),
        pltpu.VMEM(log_sum.shape[::-1], F32),
        pltpu.VMEM((2 * HALF, HD), F32),
        pltpu.VMEM((2, ROWS, HD), F32),
        pltpu.VMEM((2, ROWS, HD), F32),
        pltpu.VMEM((2, ROWS, HD), F32),
        pltpu.VMEM((2, ROWS, HD), BF16),
        pltpu.VMEM((2, ROWS, HD), BF16),
        pltpu.VMEM((2, ROWS, HD), BF16),
        pltpu.VMEM((2, ROWS, HD), BF16),
        pltpu.VMEM((2, ROWS, HD), BF16),
        pltpu.VMEM((2, 2 * HALF, HD), BF16),
        pltpu.VMEM((2, 2 * HALF, HD), BF16),
        pltpu.VMEM((2, 2, HALF, HD), BF16),
        pltpu.VMEM((2, 2, HALF, HD), BF16),
        dma((3,)),
        dma((2, BLOCKS)),
        dma((2,)),
        dma((2, BLOCKS)),
        dma((2,)),
        dma((2,)),
        dma((3,)),
        dma((2,)),
        dma((2,)),
        dma((2, BLOCKS)),
        dma((3,)),
        dma((4, 2)),
        dma((2, BLOCKS)),
        dma((2,)),
        dma((2, 2)),
        dma((SLOTS,)),
        dma((2,)),
        dma((2,)),
        dma((2,)),
        dma((2, BLOCKS)),
        dma((3,)),
    ]

    def body(*refs):
        kernel(groups, *refs)

    return pl.pallas_call(
        body,
        out_shape=(result, result, result),
        in_specs=[any_] * 6,
        out_specs=(any_, any_, any_),
        scratch_shapes=scratch,
        compiler_params=pltpu.CompilerParams(
            collective_id=0, has_side_effects=True, vmem_limit_bytes=60 * 2**20
        ),
        cost_estimate=pl.CostEstimate(flops=4 * 10**9, bytes_accessed=4 * 2**20, transcendentals=3 * 2**20),
        name="attention_backward",
    )(queries, keys, values, outputs, out_grad, jnp.transpose(log_sum))


def solution(mesh):
    spec = P(("blk", "head"), None)
    return jax.shard_map(
        per_device, mesh=mesh, in_specs=(spec,) * 6, out_specs=(spec,) * 3, check_vma=False
    )
```

```python
import math

import jax
import jax.numpy as jnp
from jax import lax
from jax.experimental import pallas as pl
from jax.experimental.pallas import tpu as pltpu
from jax.sharding import PartitionSpec as P

MESH = pl.DeviceIdType.MESH
HD = 128
SCALE = HD**-0.5
LOG2E = math.log2(math.e)
F32 = jnp.float32
BF16 = jnp.bfloat16
NX = 4
SLOTS = 2 * NX
BLOCKS = 4
ROWS = SLOTS * 128
HALF = 256


def nt(a, b, **kw):
    return lax.dot_general(a, b, (((1,), (1,)), ((), ())), preferred_element_type=F32, **kw)


def nn(a, b, **kw):
    return lax.dot_general(a, b, (((1,), (0,)), ((), ())), preferred_element_type=F32, **kw)


def tn(a, b):
    return lax.dot_general(a, b, (((0,), (0,)), ((), ())), preferred_element_type=F32)


def tile(k, v, q, g, lse, delta):
    p = jnp.exp2(nt(k, q) * (SCALE * LOG2E) - lse)
    ds = (p * (nt(v, g) - delta)).astype(BF16)
    dv = nn(p.astype(BF16), g)
    dk = nn(ds, q)
    dq = tn(ds, k)
    return dk, dv, dq


def kernel(
    groups,
    q_in, k_in, v_in, o_in, g_in, l_in,
    dq_res, dk_res, dv_res,
    qg, kv, kvp, eqg, st_all, st, est, g_v, o_v, l_v,
    dq_edge, dq_own, dk_acc, dv_acc,
    dq_oth, dq_got, dq_out, dk_out, dv_out, dqe_out, dqe_got, dkv_out, dkv_got,
    loc, r_qg, r_kv, r_b, r_k, r_c, r_st, r_dqe, r_dkv, r_d, r_out,
    s_a, s_b, s_k, s_c, s_st, s_st2, s_dqe, s_dkv, s_d, s_out,
):
    head = lax.axis_index("head")
    blk = lax.axis_index("blk")
    x = lax.div(head, 2)
    zl = lax.rem(head, 2)
    grp = lax.div(blk, 2)
    c = lax.rem(blk, 2)
    me_t = x * 2 + c
    me_s = c * NX + x
    eb = 3 * zl
    pb = 3 - eb
    partner = (x * 2 + (1 - zl), blk)
    near = (x * 2 + (1 - zl), lax.rem(grp + 2 * zl - 1 + groups, groups) * 2 + c)
    order = [pb + i * (2 * zl - 1) for i in range(BLOCKS)]
    twin = [(x, 1 - c)]
    others = [(lax.rem(x + dx, NX), cc) for dx in (1, 3, 2) for cc in range(2)]

    def device_at(xt, ct):
        return (xt * 2 + zl, grp * 2 + ct)

    def rows(b):
        return pl.ds(pl.multiple_of(b * HALF, HALF), HALF)

    def run(s):
        return pl.ds(pl.multiple_of(s * 128, 128), 128)

    def cols(t, hl):
        return pl.ds(pl.multiple_of(t * 256 + hl * 128, 128), 128)

    def remote(src, dst, ssem, rsem, device):
        copy = pltpu.make_async_remote_copy(
            src_ref=src, dst_ref=dst, send_sem=ssem, recv_sem=rsem, device_id=device, device_id_type=MESH
        )
        copy.start()
        return copy

    def arrived(ref, sem):
        pltpu.make_async_copy(ref, ref, sem).wait()

    pending = []

    def arrays(hl, which):
        if which == 0:
            sem = r_qg.at[hl, me_s]
            return ((q_in, qg.at[0, 0, hl], 0, sem), (g_in, qg.at[0, 1, hl], 1, sem))
        sem = r_kv.at[hl]
        return ((k_in, kv.at[0, hl], 2, sem), (v_in, kv.at[1, hl], 3, sem))

    for hl in range(2):
        for src, dst, _, sem in arrays(hl, 0):
            pltpu.make_async_copy(src.at[:, cols(me_t, hl)], dst.at[run(me_s)], sem).start()
    locals_ = [
        pltpu.make_async_copy(g_in, g_v, loc.at[0]),
        pltpu.make_async_copy(o_in, o_v, loc.at[1]),
        pltpu.make_async_copy(l_in, l_v, loc.at[2]),
    ]
    for copy in locals_:
        copy.start()
    for hl in range(2):
        for src, dst, _, sem in arrays(hl, 1):
            pltpu.make_async_copy(src.at[:, cols(me_t, hl)], dst.at[run(me_s)], sem).start()

    barrier = pltpu.get_barrier_semaphore()
    for device in [device_at(*t) for t in twin + others] + [partner, near]:
        pl.semaphore_signal(barrier, inc=1, device_id=device, device_id_type=MESH)
    pl.semaphore_wait(barrier, SLOTS + 1)

    def spread(hl, which, targets):
        for xt, ct in targets:
            for src, dst, n, sem in arrays(hl, which):
                remote(
                    src.at[:, cols(xt * 2 + ct, hl)], dst.at[run(me_s)], s_a.at[n, hl], sem, device_at(xt, ct)
                )

    def forward(hl, s):
        arrived(qg.at[0, :, hl, run(s)], r_qg.at[hl, s])
        pending.append(remote(
            qg.at[0, :, hl, run(s)], qg.at[1, :, hl, run(s)], s_b.at[hl, s], r_b.at[hl, lax.div(s, 2)], partner
        ))

    spread(0, 0, twin)
    spread(1, 0, twin)
    spread(0, 0, others)
    for hl in range(2):
        forward(hl, me_s)
    spread(1, 0, others)
    twin_s = (1 - c) * NX + x
    for hl in range(2):
        forward(hl, twin_s)

    for copy in locals_:
        copy.wait()
    col = lax.broadcasted_iota(jnp.int32, (SLOTS * 256, 128), 0)
    r = lax.broadcasted_iota(jnp.int32, (SLOTS * 256, 128), 1)
    wanted = lax.shift_right_logical(r, 3) * 2 + lax.shift_right_logical(r & 7, 1)
    pick = jnp.where(
        (lax.shift_right_logical(col, 7) == wanted) & ((r & 1) == 1) & ((r & 7) < 4), 1.0, 0.0
    ).astype(BF16)
    prod = g_v[...].astype(F32) * o_v[...].astype(F32)
    high = prod.astype(BF16)
    low = (prod - high.astype(F32)).astype(BF16)
    sums = nn(high, pick) + nn(low, pick)
    st_all[...] = jnp.transpose(sums)[: 8 * SLOTS]
    for h in range(2 * SLOTS):
        place = 8 * (h // 2) + 2 * (h % 2)
        st_all[place : place + 1, :] = l_v[h : h + 1, :] * LOG2E
    mine = st_all.at[pl.ds(pl.multiple_of(me_t * 8, 8), 8)]
    pltpu.make_async_copy(mine, st.at[0, me_s], r_st.at[0]).start()
    for n, (xt, ct) in enumerate(twin + others):
        pending.append(remote(
            st_all.at[pl.ds(pl.multiple_of((xt * 2 + ct) * 8, 8), 8)],
            st.at[0, me_s], s_st.at[n], r_st.at[0], device_at(xt, ct),
        ))

    rest = [cc * NX + lax.rem(x + dx, NX) for dx in (3, 1, 2) for cc in range(2)]
    for s in rest:
        forward(0, s)
    spread(0, 1, twin + others)
    spread(1, 1, twin + others)
    for s in rest[:4]:
        forward(1, s)
    arrived(st.at[0], r_st.at[0])
    pending.append(remote(st.at[0], st.at[1], s_st2.at[0], r_st.at[1], partner))
    for s in rest[4:]:
        forward(1, s)

    dk_acc[...] = jnp.zeros_like(dk_acc)
    dv_acc[...] = jnp.zeros_like(dv_acc)

    def forward_kv(hl):
        arrived(kv.at[:, hl], r_kv.at[hl])
        pending.append(remote(kv.at[:, hl, rows(pb)], kvp.at[hl], s_k.at[hl], r_k.at[hl], partner))

    def forward_edge(hl):
        pending.append(remote(
            qg.at[0, :, hl, rows(eb)], eqg.at[hl, :, pl.ds(0, HALF)], s_c.at[hl, 0], r_c.at[hl], near
        ))
        arrived(qg.at[1, :, hl, rows(eb)], r_b.at[hl, eb])
        pending.append(remote(
            qg.at[1, :, hl, rows(eb)], eqg.at[hl, :, pl.ds(HALF, HALF)], s_c.at[hl, 1], r_c.at[hl], near
        ))

    def stat(ref, parities, first, hl, n):
        place = 2 * hl + n
        return jnp.concatenate(
            [ref[p, first + j, place : place + 1, :] for p in parities for j in range(2)], axis=1
        )

    def queries(hl, parity, i):
        b = order[i]
        if parity == 1 and i < BLOCKS - 1:
            arrived(qg.at[1, :, hl, rows(b)], r_b.at[hl, b])
        count = (2 if i in (0, BLOCKS - 1) else 3) * HALF
        keys = pl.ds(pl.multiple_of(jnp.maximum(b - 1, 0) * HALF, HALF), count)
        dk, dv, dq = tile(
            kv[0, hl, keys], kv[1, hl, keys], qg[parity, 0, hl, rows(b)], qg[parity, 1, hl, rows(b)],
            stat(st, (parity,), 2 * b, hl, 0), stat(st, (parity,), 2 * b, hl, 1),
        )
        dk_acc[hl, keys] += dk
        dv_acc[hl, keys] += dv
        dq = dq * SCALE
        if parity == 0:
            dq_own[hl, rows(b)] = dq
        elif i == BLOCKS - 1:
            dq_edge[hl] = dq
        else:
            dq_oth[hl, rows(b)] = dq.astype(BF16)

    def edge(hl):
        arrived(kvp.at[hl], r_k.at[hl])
        arrived(eqg.at[hl], r_c.at[hl])
        dk, dv, dq = tile(
            jnp.concatenate([kvp[hl, 0], kv[0, hl, rows(eb)]], axis=0),
            jnp.concatenate([kvp[hl, 1], kv[1, hl, rows(eb)]], axis=0),
            eqg[hl, 0], eqg[hl, 1], stat(est, (0, 1), 0, hl, 0), stat(est, (0, 1), 0, hl, 1),
        )
        dqe_out[hl] = (dq * SCALE).astype(BF16)
        pending.append(remote(dqe_out.at[hl], dqe_got.at[hl], s_dqe.at[hl], r_dqe.at[hl], near))
        dkv_out[hl, 0] = (dk[:HALF] * SCALE).astype(BF16)
        dkv_out[hl, 1] = dv[:HALF].astype(BF16)
        dk_acc[hl, rows(eb)] += dk[HALF:]
        dv_acc[hl, rows(eb)] += dv[HALF:]

    def send_edge_keys(hl):
        pending.append(remote(dkv_out.at[hl], dkv_got.at[hl], s_dkv.at[hl], r_dkv.at[hl], partner))

    def send_queries(hl, i):
        b = order[i]
        if i == BLOCKS - 1:
            arrived(dqe_got.at[hl], r_dqe.at[hl])
            dq_oth[hl, rows(b)] = (dq_edge[hl] + dqe_got[hl, pl.ds(HALF, HALF)].astype(F32)).astype(BF16)
        pending.append(remote(
            dq_oth.at[hl, rows(b)], dq_got.at[hl, rows(b)], s_d.at[hl, b], r_d.at[hl, b], partner
        ))

    def give_back(buf, res, n, hl, b):
        for j in range(2):
            s = 2 * b + j
            src = buf.at[hl, run(s)]
            dst = res.at[:, cols(me_t, hl)]

            @pl.when(s == me_s)
            def _():
                pltpu.make_async_copy(src, dst, r_out.at[n]).start()

            @pl.when(s != me_s)
            def _():
                remote(src, dst, s_out.at[n], r_out.at[n], device_at(lax.rem(s, NX), lax.div(s, NX)))

    def finish_keys(hl, i):
        b = order[i]
        dk = dk_acc[hl, rows(b)] * SCALE
        dv = dv_acc[hl, rows(b)]
        if i == 0:
            arrived(dkv_got.at[hl], r_dkv.at[hl])
            dk = dk + dkv_got[hl, 0].astype(F32)
            dv = dv + dkv_got[hl, 1].astype(F32)
        dk_out[hl, rows(b)] = dk.astype(BF16)
        dv_out[hl, rows(b)] = dv.astype(BF16)
        give_back(dk_out, dk_res, 1, hl, b)
        give_back(dv_out, dv_res, 2, hl, b)

    def finish_queries(hl, i):
        b = order[i]
        arrived(dq_got.at[hl, rows(b)], r_d.at[hl, b])
        dq = dq_own[hl, rows(b)] + dq_got[hl, rows(b)].astype(F32)
        if i == BLOCKS - 1:
            dq = dq + dqe_got[hl, pl.ds(0, HALF)].astype(F32)
        dq_out[hl, rows(b)] = dq.astype(BF16)
        give_back(dq_out, dq_res, 0, hl, b)

    forward_edge(0)
    arrived(st.at[1], r_st.at[1])
    pending.append(remote(st.at[:, pl.ds(2 * eb, 2)], est, s_st2.at[1], r_st.at[2], near))
    forward_kv(0)
    for i in range(BLOCKS):
        queries(0, 0, i)
    for i in reversed(range(BLOCKS)):
        queries(0, 1, i)
    forward_kv(1)
    for i in (2, 1, 0):
        send_queries(0, i)
    for i in (2, 1):
        finish_keys(0, i)
    forward_edge(1)
    for i in range(BLOCKS):
        queries(1, 0, i)
    arrived(est, r_st.at[2])
    edge(0)
    send_edge_keys(0)
    finish_keys(0, 3)
    for i in (3, 2, 1, 0):
        queries(1, 1, i)
        if i < BLOCKS - 1:
            send_queries(1, i)
    for i in (2, 1):
        finish_keys(1, i)
    edge(1)
    send_edge_keys(1)
    finish_keys(1, 3)
    send_queries(0, 3)
    for i in (1, 2, 3):
        finish_queries(0, i)
    send_queries(1, 3)
    for i in (1, 2, 3):
        finish_queries(1, i)
    finish_keys(0, 0)
    finish_keys(1, 0)
    finish_queries(0, 0)
    finish_queries(1, 0)

    for copy in pending:
        copy.wait_send()
    for n in range(4):
        for hl in range(2):
            arrived(kv.at[0, 0, pl.ds(0, 7 * 128)], s_a.at[n, hl])
    for n, res in enumerate((dq_res, dk_res, dv_res)):
        arrived(dk_out.at[:, pl.ds(0, 7 * 128)], s_out.at[n])
        arrived(res, r_out.at[n])


def copy_kernel(a_ref, b_ref, c_ref, a_res, b_res, c_res, held, sems):
    refs = ((a_ref, a_res), (b_ref, b_res), (c_ref, c_res))
    loads = [pltpu.make_async_copy(src, held.at[n], sems.at[0, n]) for n, (src, _) in enumerate(refs)]
    stores = [pltpu.make_async_copy(held.at[n], dst, sems.at[1, n]) for n, (_, dst) in enumerate(refs)]
    for load in loads:
        load.start()
    for load, store in zip(loads, stores):
        load.wait()
        store.start()
    for store in stores:
        store.wait()


def per_device(queries, keys, values, outputs, out_grad, log_sum):
    groups = lax.axis_size("blk") // 2
    tokens, width = queries.shape
    any_ = pl.BlockSpec(memory_space=pl.ANY)
    dma = pltpu.SemaphoreType.DMA
    result = jax.ShapeDtypeStruct((tokens, width), BF16)
    scratch = [
        pltpu.VMEM((2, 2, 2, ROWS, HD), BF16),
        pltpu.VMEM((2, 2, ROWS, HD), BF16),
        pltpu.VMEM((2, 2, HALF, HD), BF16),
        pltpu.VMEM((2, 2, 2 * HALF, HD), BF16),
        pltpu.VMEM((8 * SLOTS, 128), F32),
        pltpu.VMEM((2, SLOTS, 8, 128), F32),
        pltpu.VMEM((2, 2, 8, 128), F32),
        pltpu.VMEM((tokens, width), BF16),
        pltpu.VMEM((tokens, width), BF16),
        pltpu.VMEM(log_sum.shape[::-1], F32),
        pltpu.VMEM((2, HALF, HD), F32),
        pltpu.VMEM((2, ROWS, HD), F32),
        pltpu.VMEM((2, ROWS, HD), F32),
        pltpu.VMEM((2, ROWS, HD), F32),
        pltpu.VMEM((2, ROWS, HD), BF16),
        pltpu.VMEM((2, ROWS, HD), BF16),
        pltpu.VMEM((2, ROWS, HD), BF16),
        pltpu.VMEM((2, ROWS, HD), BF16),
        pltpu.VMEM((2, ROWS, HD), BF16),
        pltpu.VMEM((2, 2 * HALF, HD), BF16),
        pltpu.VMEM((2, 2 * HALF, HD), BF16),
        pltpu.VMEM((2, 2, HALF, HD), BF16),
        pltpu.VMEM((2, 2, HALF, HD), BF16),
        dma((3,)),
        dma((2, SLOTS)),
        dma((2,)),
        dma((2, BLOCKS)),
        dma((2,)),
        dma((2,)),
        dma((3,)),
        dma((2,)),
        dma((2,)),
        dma((2, BLOCKS)),
        dma((3,)),
        dma((4, 2)),
        dma((2, SLOTS)),
        dma((2,)),
        dma((2, 2)),
        dma((SLOTS,)),
        dma((2,)),
        dma((2,)),
        dma((2,)),
        dma((2, BLOCKS)),
        dma((3,)),
    ]

    def body(*refs):
        kernel(groups, *refs)

    grads = pl.pallas_call(
        body,
        out_shape=(result, result, result),
        in_specs=[any_] * 6,
        out_specs=(any_, any_, any_),
        scratch_shapes=scratch,
        compiler_params=pltpu.CompilerParams(
            collective_id=0, has_side_effects=True, vmem_limit_bytes=60 * 2**20
        ),
        cost_estimate=pl.CostEstimate(flops=4 * 10**9, bytes_accessed=4 * 2**20, transcendentals=3 * 2**20),
        name="attention_backward",
    )(queries, keys, values, outputs, out_grad, jnp.transpose(log_sum))
    return pl.pallas_call(
        copy_kernel,
        out_shape=(result, result, result),
        in_specs=[any_] * 3,
        out_specs=(any_, any_, any_),
        scratch_shapes=[pltpu.VMEM((3, tokens, width), BF16), dma((2, 3))],
        compiler_params=pltpu.CompilerParams(vmem_limit_bytes=60 * 2**20),
        name="results",
    )(*grads)


def solution(mesh):
    spec = P(("blk", "head"), None)
    return jax.shard_map(
        per_device, mesh=mesh, in_specs=(spec,) * 6, out_specs=(spec,) * 3, check_vma=False
    )
```

```python
import math

import jax
import jax.numpy as jnp
from jax import lax
from jax.experimental import pallas as pl
from jax.experimental.pallas import tpu as pltpu
from jax.sharding import PartitionSpec as P

MESH = pl.DeviceIdType.MESH
HD = 128
SCALE = HD**-0.5
LOG2E = math.log2(math.e)
F32 = jnp.float32
BF16 = jnp.bfloat16
NX = 4
SLOTS = 2 * NX
BLOCKS = 4
ROWS = SLOTS * 128
HALF = 256


def nt(a, b, **kw):
    return lax.dot_general(a, b, (((1,), (1,)), ((), ())), preferred_element_type=F32, **kw)


def nn(a, b, **kw):
    return lax.dot_general(a, b, (((1,), (0,)), ((), ())), preferred_element_type=F32, **kw)


def tn(a, b):
    return lax.dot_general(a, b, (((0,), (0,)), ((), ())), preferred_element_type=F32)


def tile(k, v, q, g, lse, delta):
    p = jnp.exp2(nt(k, q) * (SCALE * LOG2E) - lse)
    ds = (p * (nt(v, g) - delta)).astype(BF16)
    dv = nn(p.astype(BF16), g)
    dk = nn(ds, q)
    dq = tn(ds, k)
    return dk, dv, dq


def kernel(
    groups,
    q_in, k_in, v_in, o_in, g_in, l_in,
    dq_res, dk_res, dv_res,
    qg, kv, kvp, eqg, st_all, st, est, g_v, o_v, l_v,
    dq_edge, dq_own, dk_acc, dv_acc,
    dq_oth, dq_got, dq_out, dk_out, dv_out, dqe_out, dqe_got, dkv_out, dkv_got,
    loc, r_qg, r_kv, r_b, r_k, r_c, r_st, r_dqe, r_dkv, r_d, r_out,
    s_a, s_b, s_k, s_c, s_st, s_st2, s_dqe, s_dkv, s_d, s_out,
):
    head = lax.axis_index("head")
    blk = lax.axis_index("blk")
    x = lax.div(head, 2)
    zl = lax.rem(head, 2)
    grp = lax.div(blk, 2)
    c = lax.rem(blk, 2)
    me_t = x * 2 + c
    me_s = c * NX + x
    eb = 3 * zl
    pb = 3 - eb
    partner = (x * 2 + (1 - zl), blk)
    near = (x * 2 + (1 - zl), lax.rem(grp + 2 * zl - 1 + groups, groups) * 2 + c)
    order = [pb + i * (2 * zl - 1) for i in range(BLOCKS)]
    twin = [(x, 1 - c)]
    others = [(lax.rem(x + dx, NX), cc) for dx in (1, 3, 2) for cc in range(2)]

    def device_at(xt, ct):
        return (xt * 2 + zl, grp * 2 + ct)

    def rows(b):
        return pl.ds(pl.multiple_of(b * HALF, HALF), HALF)

    def run(s):
        return pl.ds(pl.multiple_of(s * 128, 128), 128)

    def cols(t, hl):
        return pl.ds(pl.multiple_of(t * 256 + hl * 128, 128), 128)

    def remote(src, dst, ssem, rsem, device):
        copy = pltpu.make_async_remote_copy(
            src_ref=src, dst_ref=dst, send_sem=ssem, recv_sem=rsem, device_id=device, device_id_type=MESH
        )
        copy.start()
        return copy

    def arrived(ref, sem):
        pltpu.make_async_copy(ref, ref, sem).wait()

    pending = []

    def arrays(hl, which):
        if which == 0:
            sem = r_qg.at[hl, me_s]
            return ((q_in, qg.at[0, 0, hl], 0, sem), (g_in, qg.at[0, 1, hl], 1, sem))
        sem = r_kv.at[hl]
        return ((k_in, kv.at[0, hl], 2, sem), (v_in, kv.at[1, hl], 3, sem))

    for hl in range(2):
        for src, dst, _, sem in arrays(hl, 0):
            pltpu.make_async_copy(src.at[:, cols(me_t, hl)], dst.at[run(me_s)], sem).start()
    locals_ = [
        pltpu.make_async_copy(g_in, g_v, loc.at[0]),
        pltpu.make_async_copy(o_in, o_v, loc.at[1]),
        pltpu.make_async_copy(l_in, l_v, loc.at[2]),
    ]
    for copy in locals_:
        copy.start()
    for hl in range(2):
        for src, dst, _, sem in arrays(hl, 1):
            pltpu.make_async_copy(src.at[:, cols(me_t, hl)], dst.at[run(me_s)], sem).start()

    barrier = pltpu.get_barrier_semaphore()
    for device in [device_at(*t) for t in twin + others] + [partner, near]:
        pl.semaphore_signal(barrier, inc=1, device_id=device, device_id_type=MESH)
    pl.semaphore_wait(barrier, SLOTS + 1)

    def spread(hl, which, targets):
        for xt, ct in targets:
            for src, dst, n, sem in arrays(hl, which):
                remote(
                    src.at[:, cols(xt * 2 + ct, hl)], dst.at[run(me_s)], s_a.at[n, hl], sem, device_at(xt, ct)
                )

    def forward(hl, s):
        arrived(qg.at[0, :, hl, run(s)], r_qg.at[hl, s])
        pending.append(remote(
            qg.at[0, :, hl, run(s)], qg.at[1, :, hl, run(s)], s_b.at[hl, s], r_b.at[hl, lax.div(s, 2)], partner
        ))

    spread(0, 0, twin)
    spread(1, 0, twin)
    spread(0, 0, others)
    for hl in range(2):
        forward(hl, me_s)
    twin_s = (1 - c) * NX + x
    for hl in range(2):
        forward(hl, twin_s)

    for copy in locals_:
        copy.wait()
    col = lax.broadcasted_iota(jnp.int32, (SLOTS * 256, 128), 0)
    r = lax.broadcasted_iota(jnp.int32, (SLOTS * 256, 128), 1)
    wanted = lax.shift_right_logical(r, 3) * 2 + lax.shift_right_logical(r & 7, 1)
    pick = jnp.where(
        (lax.shift_right_logical(col, 7) == wanted) & ((r & 1) == 1) & ((r & 7) < 4), 1.0, 0.0
    ).astype(BF16)
    prod = g_v[...].astype(F32) * o_v[...].astype(F32)
    high = prod.astype(BF16)
    low = (prod - high.astype(F32)).astype(BF16)
    sums = nn(high, pick) + nn(low, pick)
    st_all[...] = jnp.transpose(sums)[: 8 * SLOTS]
    for h in range(2 * SLOTS):
        place = 8 * (h // 2) + 2 * (h % 2)
        st_all[place : place + 1, :] = l_v[h : h + 1, :] * LOG2E
    mine = st_all.at[pl.ds(pl.multiple_of(me_t * 8, 8), 8)]
    pltpu.make_async_copy(mine, st.at[0, me_s], r_st.at[0]).start()
    for n, (xt, ct) in enumerate(twin + others):
        pending.append(remote(
            st_all.at[pl.ds(pl.multiple_of((xt * 2 + ct) * 8, 8), 8)],
            st.at[0, me_s], s_st.at[n], r_st.at[0], device_at(xt, ct),
        ))

    spread(0, 1, twin + others)

    rest = [cc * NX + lax.rem(x + dx, NX) for dx in (3, 1, 2) for cc in range(2)]
    for s in rest[:4]:
        forward(0, s)
    spread(1, 0, others)
    arrived(st.at[0], r_st.at[0])
    pending.append(remote(st.at[0], st.at[1], s_st2.at[0], r_st.at[1], partner))
    for s in rest[4:]:
        forward(0, s)
    spread(1, 1, twin + others)

    dk_acc[...] = jnp.zeros_like(dk_acc)
    dv_acc[...] = jnp.zeros_like(dv_acc)

    def forward_kv(hl):
        arrived(kv.at[:, hl], r_kv.at[hl])
        pending.append(remote(kv.at[:, hl, rows(pb)], kvp.at[hl], s_k.at[hl], r_k.at[hl], partner))

    def forward_own_edge(hl):
        pending.append(remote(
            qg.at[0, :, hl, rows(eb)], eqg.at[hl, :, pl.ds(0, HALF)], s_c.at[hl, 0], r_c.at[hl], near
        ))

    def forward_edge(hl):
        arrived(qg.at[1, :, hl, rows(eb)], r_b.at[hl, eb])
        pending.append(remote(
            qg.at[1, :, hl, rows(eb)], eqg.at[hl, :, pl.ds(HALF, HALF)], s_c.at[hl, 1], r_c.at[hl], near
        ))

    def stat(ref, parities, first, hl, n):
        place = 2 * hl + n
        return jnp.concatenate(
            [ref[p, first + j, place : place + 1, :] for p in parities for j in range(2)], axis=1
        )

    def queries(hl, parity, i):
        b = order[i]
        if parity == 1 and i < BLOCKS - 1:
            arrived(qg.at[1, :, hl, rows(b)], r_b.at[hl, b])
        count = (2 if i in (0, BLOCKS - 1) else 3) * HALF
        keys = pl.ds(pl.multiple_of(jnp.maximum(b - 1, 0) * HALF, HALF), count)
        dk, dv, dq = tile(
            kv[0, hl, keys], kv[1, hl, keys], qg[parity, 0, hl, rows(b)], qg[parity, 1, hl, rows(b)],
            stat(st, (parity,), 2 * b, hl, 0), stat(st, (parity,), 2 * b, hl, 1),
        )
        dk_acc[hl, keys] += dk
        dv_acc[hl, keys] += dv
        dq = dq * SCALE
        if parity == 0:
            dq_own[hl, rows(b)] = dq
        elif i == BLOCKS - 1:
            dq_edge[hl] = dq
        else:
            dq_oth[hl, rows(b)] = dq.astype(BF16)

    def edge(hl):
        arrived(kvp.at[hl], r_k.at[hl])
        arrived(eqg.at[hl], r_c.at[hl])
        dk, dv, dq = tile(
            jnp.concatenate([kvp[hl, 0], kv[0, hl, rows(eb)]], axis=0),
            jnp.concatenate([kvp[hl, 1], kv[1, hl, rows(eb)]], axis=0),
            eqg[hl, 0], eqg[hl, 1], stat(est, (0, 1), 0, hl, 0), stat(est, (0, 1), 0, hl, 1),
        )
        dqe_out[hl] = (dq * SCALE).astype(BF16)
        pending.append(remote(dqe_out.at[hl], dqe_got.at[hl], s_dqe.at[hl], r_dqe.at[hl], near))
        dkv_out[hl, 0] = (dk[:HALF] * SCALE).astype(BF16)
        dkv_out[hl, 1] = dv[:HALF].astype(BF16)
        dk_acc[hl, rows(eb)] += dk[HALF:]
        dv_acc[hl, rows(eb)] += dv[HALF:]

    def send_edge_keys(hl):
        pending.append(remote(dkv_out.at[hl], dkv_got.at[hl], s_dkv.at[hl], r_dkv.at[hl], partner))

    def send_queries(hl, i):
        b = order[i]
        if i == BLOCKS - 1:
            arrived(dqe_got.at[hl], r_dqe.at[hl])
            dq_oth[hl, rows(b)] = (dq_edge[hl] + dqe_got[hl, pl.ds(HALF, HALF)].astype(F32)).astype(BF16)
        pending.append(remote(
            dq_oth.at[hl, rows(b)], dq_got.at[hl, rows(b)], s_d.at[hl, b], r_d.at[hl, b], partner
        ))

    def give_back(buf, res, n, hl, b):
        for j in range(2):
            s = 2 * b + j
            src = buf.at[hl, run(s)]
            dst = res.at[:, cols(me_t, hl)]

            @pl.when(s == me_s)
            def _():
                pltpu.make_async_copy(src, dst, r_out.at[n]).start()

            @pl.when(s != me_s)
            def _():
                remote(src, dst, s_out.at[n], r_out.at[n], device_at(lax.rem(s, NX), lax.div(s, NX)))

    def finish_keys(hl, i):
        b = order[i]
        dk = dk_acc[hl, rows(b)] * SCALE
        dv = dv_acc[hl, rows(b)]
        if i == 0:
            arrived(dkv_got.at[hl], r_dkv.at[hl])
            dk = dk + dkv_got[hl, 0].astype(F32)
            dv = dv + dkv_got[hl, 1].astype(F32)
        dk_out[hl, rows(b)] = dk.astype(BF16)
        dv_out[hl, rows(b)] = dv.astype(BF16)
        give_back(dk_out, dk_res, 1, hl, b)
        give_back(dv_out, dv_res, 2, hl, b)

    def finish_queries(hl, i):
        b = order[i]
        arrived(dq_got.at[hl, rows(b)], r_d.at[hl, b])
        dq = dq_own[hl, rows(b)] + dq_got[hl, rows(b)].astype(F32)
        if i == BLOCKS - 1:
            dq = dq + dqe_got[hl, pl.ds(0, HALF)].astype(F32)
        dq_out[hl, rows(b)] = dq.astype(BF16)
        give_back(dq_out, dq_res, 0, hl, b)

    forward_own_edge(0)
    forward_kv(0)
    for i in range(BLOCKS):
        queries(0, 0, i)
    for s in rest[:4]:
        forward(1, s)
    forward_edge(0)
    arrived(st.at[1], r_st.at[1])
    pending.append(remote(st.at[:, pl.ds(2 * eb, 2)], est, s_st2.at[1], r_st.at[2], near))
    for i in (3, 2):
        queries(0, 1, i)
    for s in rest[4:]:
        forward(1, s)
    forward_own_edge(1)
    for i in (1, 0):
        queries(0, 1, i)
    arrived(est, r_st.at[2])
    edge(0)
    for i in (2, 1, 3):
        finish_keys(0, i)
    forward_edge(1)
    forward_kv(1)
    for i in (2, 1, 0):
        send_queries(0, i)
    send_edge_keys(0)
    for i in range(BLOCKS):
        queries(1, 0, i)
    send_queries(0, 3)
    for i in (3, 2):
        queries(1, 1, i)
    edge(1)
    send_edge_keys(1)
    send_queries(1, 2)
    for i in (1, 0):
        queries(1, 1, i)
        send_queries(1, i)
    for i in (2, 1, 3):
        finish_keys(1, i)
    for i in (1, 2, 3):
        finish_queries(0, i)
    finish_keys(0, 0)
    send_queries(1, 3)
    finish_queries(0, 0)
    finish_keys(1, 0)
    for i in (1, 2, 3):
        finish_queries(1, i)
    finish_queries(1, 0)

    for copy in pending:
        copy.wait_send()
    for n in range(4):
        for hl in range(2):
            arrived(kv.at[0, 0, pl.ds(0, 7 * 128)], s_a.at[n, hl])
    for n, res in enumerate((dq_res, dk_res, dv_res)):
        arrived(dk_out.at[:, pl.ds(0, 7 * 128)], s_out.at[n])
        arrived(res, r_out.at[n])


def copy_kernel(a_ref, b_ref, c_ref, a_res, b_res, c_res, held, sems):
    refs = ((a_ref, a_res), (b_ref, b_res), (c_ref, c_res))
    loads = [pltpu.make_async_copy(src, held.at[n], sems.at[0, n]) for n, (src, _) in enumerate(refs)]
    stores = [pltpu.make_async_copy(held.at[n], dst, sems.at[1, n]) for n, (_, dst) in enumerate(refs)]
    for load in loads:
        load.start()
    for load, store in zip(loads, stores):
        load.wait()
        store.start()
    for store in stores:
        store.wait()


def per_device(queries, keys, values, outputs, out_grad, log_sum):
    groups = lax.axis_size("blk") // 2
    tokens, width = queries.shape
    any_ = pl.BlockSpec(memory_space=pl.ANY)
    dma = pltpu.SemaphoreType.DMA
    result = jax.ShapeDtypeStruct((tokens, width), BF16)
    scratch = [
        pltpu.VMEM((2, 2, 2, ROWS, HD), BF16),
        pltpu.VMEM((2, 2, ROWS, HD), BF16),
        pltpu.VMEM((2, 2, HALF, HD), BF16),
        pltpu.VMEM((2, 2, 2 * HALF, HD), BF16),
        pltpu.VMEM((8 * SLOTS, 128), F32),
        pltpu.VMEM((2, SLOTS, 8, 128), F32),
        pltpu.VMEM((2, 2, 8, 128), F32),
        pltpu.VMEM((tokens, width), BF16),
        pltpu.VMEM((tokens, width), BF16),
        pltpu.VMEM(log_sum.shape[::-1], F32),
        pltpu.VMEM((2, HALF, HD), F32),
        pltpu.VMEM((2, ROWS, HD), F32),
        pltpu.VMEM((2, ROWS, HD), F32),
        pltpu.VMEM((2, ROWS, HD), F32),
        pltpu.VMEM((2, ROWS, HD), BF16),
        pltpu.VMEM((2, ROWS, HD), BF16),
        pltpu.VMEM((2, ROWS, HD), BF16),
        pltpu.VMEM((2, ROWS, HD), BF16),
        pltpu.VMEM((2, ROWS, HD), BF16),
        pltpu.VMEM((2, 2 * HALF, HD), BF16),
        pltpu.VMEM((2, 2 * HALF, HD), BF16),
        pltpu.VMEM((2, 2, HALF, HD), BF16),
        pltpu.VMEM((2, 2, HALF, HD), BF16),
        dma((3,)),
        dma((2, SLOTS)),
        dma((2,)),
        dma((2, BLOCKS)),
        dma((2,)),
        dma((2,)),
        dma((3,)),
        dma((2,)),
        dma((2,)),
        dma((2, BLOCKS)),
        dma((3,)),
        dma((4, 2)),
        dma((2, SLOTS)),
        dma((2,)),
        dma((2, 2)),
        dma((SLOTS,)),
        dma((2,)),
        dma((2,)),
        dma((2,)),
        dma((2, BLOCKS)),
        dma((3,)),
    ]

    def body(*refs):
        kernel(groups, *refs)

    grads = pl.pallas_call(
        body,
        out_shape=(result, result, result),
        in_specs=[any_] * 6,
        out_specs=(any_, any_, any_),
        scratch_shapes=scratch,
        compiler_params=pltpu.CompilerParams(
            collective_id=0, has_side_effects=True, vmem_limit_bytes=60 * 2**20
        ),
        cost_estimate=pl.CostEstimate(flops=4 * 10**9, bytes_accessed=4 * 2**20, transcendentals=3 * 2**20),
        name="attention_backward",
    )(queries, keys, values, outputs, out_grad, jnp.transpose(log_sum))
    return pl.pallas_call(
        copy_kernel,
        out_shape=(result, result, result),
        in_specs=[any_] * 3,
        out_specs=(any_, any_, any_),
        scratch_shapes=[pltpu.VMEM((3, tokens, width), BF16), dma((2, 3))],
        compiler_params=pltpu.CompilerParams(vmem_limit_bytes=60 * 2**20),
        name="results",
    )(*grads)


def solution(mesh):
    spec = P(("blk", "head"), None)
    return jax.shard_map(
        per_device, mesh=mesh, in_specs=(spec,) * 6, out_specs=(spec,) * 3, check_vma=False
    )
```

```python
import math

import jax
import jax.numpy as jnp
from jax import lax
from jax.experimental import pallas as pl
from jax.experimental.pallas import tpu as pltpu
from jax.sharding import PartitionSpec as P

MESH = pl.DeviceIdType.MESH
HD = 128
SCALE = HD**-0.5
LOG2E = math.log2(math.e)
F32 = jnp.float32
BF16 = jnp.bfloat16
NX = 4
SLOTS = 2 * NX
BLOCKS = 4
ROWS = SLOTS * 128
HALF = 256


def nt(a, b, **kw):
    return lax.dot_general(a, b, (((1,), (1,)), ((), ())), preferred_element_type=F32, **kw)


def nn(a, b, **kw):
    return lax.dot_general(a, b, (((1,), (0,)), ((), ())), preferred_element_type=F32, **kw)


def tn(a, b):
    return lax.dot_general(a, b, (((0,), (0,)), ((), ())), preferred_element_type=F32)


def tile(k, v, q, g, lse, delta):
    p = jnp.exp2(nt(k, q) * (SCALE * LOG2E) - lse)
    ds = (p * (nt(v, g) - delta)).astype(BF16)
    dv = nn(p.astype(BF16), g)
    dk = nn(ds, q)
    dq = tn(ds, k)
    return dk, dv, dq


def kernel(
    groups,
    q_in, k_in, v_in, o_in, g_in, l_in,
    dq_res, dk_res, dv_res,
    qg, kv, kvp, eqg, st_all, st, est, g_v, o_v, l_v,
    dq_edge, dq_own, dk_acc, dv_acc,
    dq_oth, dq_got, dq_out, dk_out, dv_out, dqe_out, dqe_got, dkv_out, dkv_got,
    loc, r_qg, r_kv, r_b, r_k, r_c, r_st, r_dqe, r_dkv, r_d, r_out,
    s_a, s_b, s_k, s_c, s_st, s_st2, s_dqe, s_dkv, s_d, s_out, s_dl, r_dl,
):
    head = lax.axis_index("head")
    blk = lax.axis_index("blk")
    x = lax.div(head, 2)
    zl = lax.rem(head, 2)
    grp = lax.div(blk, 2)
    c = lax.rem(blk, 2)
    me_t = x * 2 + c
    me_s = c * NX + x
    eb = 3 * zl
    pb = 3 - eb
    partner = (x * 2 + (1 - zl), blk)
    near = (x * 2 + (1 - zl), lax.rem(grp + 2 * zl - 1 + groups, groups) * 2 + c)
    order = [pb + i * (2 * zl - 1) for i in range(BLOCKS)]
    twin = [(x, 1 - c)]
    others = [(lax.rem(x + dx, NX), cc) for dx in (1, 3, 2) for cc in range(2)]

    def device_at(xt, ct):
        return (xt * 2 + zl, grp * 2 + ct)

    def rows(b):
        return pl.ds(pl.multiple_of(b * HALF, HALF), HALF)

    def run(s):
        return pl.ds(pl.multiple_of(s * 128, 128), 128)

    def cols(t, hl):
        return pl.ds(pl.multiple_of(t * 256 + hl * 128, 128), 128)

    def remote(src, dst, ssem, rsem, device):
        copy = pltpu.make_async_remote_copy(
            src_ref=src, dst_ref=dst, send_sem=ssem, recv_sem=rsem, device_id=device, device_id_type=MESH
        )
        copy.start()
        return copy

    def arrived(ref, sem):
        pltpu.make_async_copy(ref, ref, sem).wait()

    pending = []

    def arrays(hl, which):
        if which == 0:
            sem = r_qg.at[hl, me_s]
            return ((q_in, qg.at[0, 0, hl], 0, sem), (g_in, qg.at[0, 1, hl], 1, sem))
        sem = r_kv.at[hl]
        return ((k_in, kv.at[0, hl], 2, sem), (v_in, kv.at[1, hl], 3, sem))

    for hl in range(2):
        for src, dst, _, sem in arrays(hl, 0):
            pltpu.make_async_copy(src.at[:, cols(me_t, hl)], dst.at[run(me_s)], sem).start()
    locals_ = [
        pltpu.make_async_copy(g_in, g_v, loc.at[0]),
        pltpu.make_async_copy(o_in, o_v, loc.at[1]),
        pltpu.make_async_copy(l_in, l_v, loc.at[2]),
    ]
    for copy in locals_:
        copy.start()
    for hl in range(2):
        for src, dst, _, sem in arrays(hl, 1):
            pltpu.make_async_copy(src.at[:, cols(me_t, hl)], dst.at[run(me_s)], sem).start()

    barrier = pltpu.get_barrier_semaphore()
    for device in [device_at(*t) for t in twin + others] + [partner, near]:
        pl.semaphore_signal(barrier, inc=1, device_id=device, device_id_type=MESH)
    pl.semaphore_wait(barrier, SLOTS + 1)

    def spread(hl, which, targets):
        for xt, ct in targets:
            for src, dst, n, sem in arrays(hl, which):
                remote(
                    src.at[:, cols(xt * 2 + ct, hl)], dst.at[run(me_s)], s_a.at[n, hl], sem, device_at(xt, ct)
                )

    def forward(hl, s):
        arrived(qg.at[0, :, hl, run(s)], r_qg.at[hl, s])
        pending.append(remote(
            qg.at[0, :, hl, run(s)], qg.at[1, :, hl, run(s)], s_b.at[hl, s], r_b.at[hl, lax.div(s, 2)], partner
        ))

    forward(0, me_s)
    spread(0, 0, twin)
    spread(0, 0, others)
    spread(1, 0, twin)
    forward(1, me_s)
    twin_s = (1 - c) * NX + x
    for hl in range(2):
        forward(hl, twin_s)

    for copy in locals_:
        copy.wait()
    col = lax.broadcasted_iota(jnp.int32, (SLOTS * 256, 128), 0)
    r = lax.broadcasted_iota(jnp.int32, (SLOTS * 256, 128), 1)
    wanted = lax.shift_right_logical(r, 3) * 2 + lax.shift_right_logical(r & 7, 1)
    pick = jnp.where(
        (lax.shift_right_logical(col, 7) == wanted) & ((r & 1) == 1) & ((r & 7) < 4), 1.0, 0.0
    ).astype(BF16)
    prod = g_v[...].astype(F32) * o_v[...].astype(F32)
    high = prod.astype(BF16)
    low = (prod - high.astype(F32)).astype(BF16)
    sums = nn(high, pick) + nn(low, pick)
    st_all[...] = jnp.transpose(sums)[: 8 * SLOTS]
    for h in range(2 * SLOTS):
        place = 8 * (h // 2) + 2 * (h % 2)
        st_all[place : place + 1, :] = l_v[h : h + 1, :] * LOG2E
    mine = st_all.at[pl.ds(pl.multiple_of(me_t * 8, 8), 8)]
    pltpu.make_async_copy(mine, st.at[0, me_s], r_st.at[0]).start()
    for n, (xt, ct) in enumerate(twin + others):
        pending.append(remote(
            st_all.at[pl.ds(pl.multiple_of((xt * 2 + ct) * 8, 8), 8)],
            st.at[0, me_s], s_st.at[n], r_st.at[0], device_at(xt, ct),
        ))

    spread(0, 1, twin + others)

    rest = [cc * NX + lax.rem(x + dx, NX) for dx in (3, 1, 2) for cc in range(2)]
    for s in rest[:4]:
        forward(0, s)
    spread(1, 0, others)
    arrived(st.at[0], r_st.at[0])
    pending.append(remote(st.at[0], st.at[1], s_st2.at[0], r_st.at[1], partner))
    for s in rest[4:]:
        forward(0, s)
    spread(1, 1, twin + others)

    dk_acc[...] = jnp.zeros_like(dk_acc)
    dv_acc[...] = jnp.zeros_like(dv_acc)

    def forward_kv(hl):
        arrived(kv.at[:, hl], r_kv.at[hl])
        pending.append(remote(kv.at[:, hl, rows(pb)], kvp.at[hl], s_k.at[hl], r_k.at[hl], partner))

    def forward_own_edge(hl):
        pending.append(remote(
            qg.at[0, :, hl, rows(eb)], eqg.at[hl, :, pl.ds(0, HALF)], s_c.at[hl, 0], r_c.at[hl], near
        ))

    def forward_edge(hl):
        arrived(qg.at[1, :, hl, rows(eb)], r_b.at[hl, eb])
        pending.append(remote(
            qg.at[1, :, hl, rows(eb)], eqg.at[hl, :, pl.ds(HALF, HALF)], s_c.at[hl, 1], r_c.at[hl], near
        ))

    def stat(ref, parities, first, hl, n):
        place = 2 * hl + n
        return jnp.concatenate(
            [ref[p, first + j, place : place + 1, :] for p in parities for j in range(2)], axis=1
        )

    def queries(hl, parity, i):
        b = order[i]
        if parity == 1 and i < BLOCKS - 1:
            arrived(qg.at[1, :, hl, rows(b)], r_b.at[hl, b])
        count = (2 if i in (0, BLOCKS - 1) else 3) * HALF
        keys = pl.ds(pl.multiple_of(jnp.maximum(b - 1, 0) * HALF, HALF), count)
        dk, dv, dq = tile(
            kv[0, hl, keys], kv[1, hl, keys], qg[parity, 0, hl, rows(b)], qg[parity, 1, hl, rows(b)],
            stat(st, (parity,), 2 * b, hl, 0), stat(st, (parity,), 2 * b, hl, 1),
        )
        dk_acc[hl, keys] += dk
        dv_acc[hl, keys] += dv
        dq = dq * SCALE
        if parity == 0:
            dq_own[hl, rows(b)] = dq
        elif i == BLOCKS - 1:
            dq_edge[hl] = dq
        else:
            dq_oth[hl, rows(b)] = dq.astype(BF16)

    def edge(hl):
        arrived(kvp.at[hl], r_k.at[hl])
        arrived(eqg.at[hl], r_c.at[hl])
        dk, dv, dq = tile(
            jnp.concatenate([kvp[hl, 0], kv[0, hl, rows(eb)]], axis=0),
            jnp.concatenate([kvp[hl, 1], kv[1, hl, rows(eb)]], axis=0),
            eqg[hl, 0], eqg[hl, 1], stat(est, (0, 1), 0, hl, 0), stat(est, (0, 1), 0, hl, 1),
        )
        dqe_out[hl] = (dq * SCALE).astype(BF16)
        pending.append(remote(dqe_out.at[hl], dqe_got.at[hl], s_dqe.at[hl], r_dqe.at[hl], near))
        dkv_out[hl, 0] = (dk[:HALF] * SCALE).astype(BF16)
        dkv_out[hl, 1] = dv[:HALF].astype(BF16)
        dk_acc[hl, rows(eb)] += dk[HALF:]
        dv_acc[hl, rows(eb)] += dv[HALF:]

    def send_edge_keys(hl):
        pending.append(remote(dkv_out.at[hl], dkv_got.at[hl], s_dkv.at[hl], r_dkv.at[hl], partner))

    def send_queries(hl, i):
        b = order[i]
        if i == BLOCKS - 1:
            arrived(dqe_got.at[hl], r_dqe.at[hl])
            dq_oth[hl, rows(b)] = (dq_edge[hl] + dqe_got[hl, pl.ds(HALF, HALF)].astype(F32)).astype(BF16)
        if hl == 1 and i == BLOCKS - 1:
            for j in range(2):
                pending.append(remote(
                    dq_oth.at[hl, run(2 * b + j)], dq_got.at[hl, run(2 * b + j)], s_dl.at[j], r_dl.at[j], partner
                ))
        else:
            pending.append(remote(
                dq_oth.at[hl, rows(b)], dq_got.at[hl, rows(b)], s_d.at[hl, b], r_d.at[hl, b], partner
            ))

    def give_back(buf, res, n, hl, b, runs=(0, 1)):
        for j in runs:
            s = 2 * b + j
            src = buf.at[hl, run(s)]
            dst = res.at[:, cols(me_t, hl)]

            @pl.when(s == me_s)
            def _():
                pltpu.make_async_copy(src, dst, r_out.at[n]).start()

            @pl.when(s != me_s)
            def _():
                remote(src, dst, s_out.at[n], r_out.at[n], device_at(lax.rem(s, NX), lax.div(s, NX)))

    def finish_keys(hl, i):
        b = order[i]
        dk = dk_acc[hl, rows(b)] * SCALE
        dv = dv_acc[hl, rows(b)]
        if i == 0:
            arrived(dkv_got.at[hl], r_dkv.at[hl])
            dk = dk + dkv_got[hl, 0].astype(F32)
            dv = dv + dkv_got[hl, 1].astype(F32)
        dk_out[hl, rows(b)] = dk.astype(BF16)
        dv_out[hl, rows(b)] = dv.astype(BF16)
        give_back(dk_out, dk_res, 1, hl, b)
        give_back(dv_out, dv_res, 2, hl, b)

    def finish_last():
        for j in range(2):
            s = 2 * order[0] + j
            arrived(dq_got.at[1, run(s)], r_dl.at[j])
            dq_out[1, run(s)] = (dq_own[1, run(s)] + dq_got[1, run(s)].astype(F32)).astype(BF16)
            give_back(dq_out, dq_res, 0, 1, order[0], (j,))

    def finish_queries(hl, i):
        b = order[i]
        arrived(dq_got.at[hl, rows(b)], r_d.at[hl, b])
        dq = dq_own[hl, rows(b)] + dq_got[hl, rows(b)].astype(F32)
        if i == BLOCKS - 1:
            dq = dq + dqe_got[hl, pl.ds(0, HALF)].astype(F32)
        dq_out[hl, rows(b)] = dq.astype(BF16)
        give_back(dq_out, dq_res, 0, hl, b)

    forward_own_edge(0)
    forward_kv(0)
    for i in range(BLOCKS):
        queries(0, 0, i)
    for s in rest[:4]:
        forward(1, s)
    forward_edge(0)
    arrived(st.at[1], r_st.at[1])
    pending.append(remote(st.at[:, pl.ds(2 * eb, 2)], est, s_st2.at[1], r_st.at[2], near))
    for i in (3, 2):
        queries(0, 1, i)
    for s in rest[4:]:
        forward(1, s)
    forward_own_edge(1)
    for i in (1, 0):
        queries(0, 1, i)
    arrived(est, r_st.at[2])
    edge(0)
    for i in (2, 1, 3):
        finish_keys(0, i)
    send_queries(0, 2)
    forward_edge(1)
    forward_kv(1)
    for i in (1, 0):
        send_queries(0, i)
    send_edge_keys(0)
    for i in range(BLOCKS):
        queries(1, 0, i)
    send_queries(0, 3)
    for i in (3, 2):
        queries(1, 1, i)
    edge(1)
    send_edge_keys(1)
    send_queries(1, 2)
    for i in (1, 0):
        queries(1, 1, i)
        send_queries(1, i)
    for i in (2, 1, 3):
        finish_keys(1, i)
    for i in (1, 2, 3):
        finish_queries(0, i)
    finish_keys(0, 0)
    send_queries(1, 3)
    finish_queries(0, 0)
    finish_keys(1, 0)
    for i in (1, 2, 3):
        finish_queries(1, i)
    finish_last()

    for copy in pending:
        copy.wait_send()
    for n in range(4):
        for hl in range(2):
            arrived(kv.at[0, 0, pl.ds(0, 7 * 128)], s_a.at[n, hl])
    for n, res in enumerate((dq_res, dk_res, dv_res)):
        arrived(dk_out.at[:, pl.ds(0, 7 * 128)], s_out.at[n])
        arrived(res, r_out.at[n])


def copy_kernel(a_ref, b_ref, c_ref, a_res, b_res, c_res, held, sems):
    refs = ((a_ref, a_res), (b_ref, b_res), (c_ref, c_res))
    loads = [pltpu.make_async_copy(src, held.at[n], sems.at[0, n]) for n, (src, _) in enumerate(refs)]
    stores = [pltpu.make_async_copy(held.at[n], dst, sems.at[1, n]) for n, (_, dst) in enumerate(refs)]
    for load in loads:
        load.start()
    for load, store in zip(loads, stores):
        load.wait()
        store.start()
    for store in stores:
        store.wait()


def per_device(queries, keys, values, outputs, out_grad, log_sum):
    groups = lax.axis_size("blk") // 2
    tokens, width = queries.shape
    any_ = pl.BlockSpec(memory_space=pl.ANY)
    dma = pltpu.SemaphoreType.DMA
    result = jax.ShapeDtypeStruct((tokens, width), BF16)
    scratch = [
        pltpu.VMEM((2, 2, 2, ROWS, HD), BF16),
        pltpu.VMEM((2, 2, ROWS, HD), BF16),
        pltpu.VMEM((2, 2, HALF, HD), BF16),
        pltpu.VMEM((2, 2, 2 * HALF, HD), BF16),
        pltpu.VMEM((8 * SLOTS, 128), F32),
        pltpu.VMEM((2, SLOTS, 8, 128), F32),
        pltpu.VMEM((2, 2, 8, 128), F32),
        pltpu.VMEM((tokens, width), BF16),
        pltpu.VMEM((tokens, width), BF16),
        pltpu.VMEM(log_sum.shape[::-1], F32),
        pltpu.VMEM((2, HALF, HD), F32),
        pltpu.VMEM((2, ROWS, HD), F32),
        pltpu.VMEM((2, ROWS, HD), F32),
        pltpu.VMEM((2, ROWS, HD), F32),
        pltpu.VMEM((2, ROWS, HD), BF16),
        pltpu.VMEM((2, ROWS, HD), BF16),
        pltpu.VMEM((2, ROWS, HD), BF16),
        pltpu.VMEM((2, ROWS, HD), BF16),
        pltpu.VMEM((2, ROWS, HD), BF16),
        pltpu.VMEM((2, 2 * HALF, HD), BF16),
        pltpu.VMEM((2, 2 * HALF, HD), BF16),
        pltpu.VMEM((2, 2, HALF, HD), BF16),
        pltpu.VMEM((2, 2, HALF, HD), BF16),
        dma((3,)),
        dma((2, SLOTS)),
        dma((2,)),
        dma((2, BLOCKS)),
        dma((2,)),
        dma((2,)),
        dma((3,)),
        dma((2,)),
        dma((2,)),
        dma((2, BLOCKS)),
        dma((3,)),
        dma((4, 2)),
        dma((2, SLOTS)),
        dma((2,)),
        dma((2, 2)),
        dma((SLOTS,)),
        dma((2,)),
        dma((2,)),
        dma((2,)),
        dma((2, BLOCKS)),
        dma((3,)),
        dma((2,)),
        dma((2,)),
    ]

    def body(*refs):
        kernel(groups, *refs)

    grads = pl.pallas_call(
        body,
        out_shape=(result, result, result),
        in_specs=[any_] * 6,
        out_specs=(any_, any_, any_),
        scratch_shapes=scratch,
        compiler_params=pltpu.CompilerParams(
            collective_id=0, has_side_effects=True, vmem_limit_bytes=60 * 2**20
        ),
        cost_estimate=pl.CostEstimate(flops=4 * 10**9, bytes_accessed=4 * 2**20, transcendentals=3 * 2**20),
        name="attention_backward",
    )(queries, keys, values, outputs, out_grad, jnp.transpose(log_sum))
    return pl.pallas_call(
        copy_kernel,
        out_shape=(result, result, result),
        in_specs=[any_] * 3,
        out_specs=(any_, any_, any_),
        scratch_shapes=[pltpu.VMEM((3, tokens, width), BF16), dma((2, 3))],
        compiler_params=pltpu.CompilerParams(vmem_limit_bytes=60 * 2**20),
        name="results",
    )(*grads)


def solution(mesh):
    spec = P(("blk", "head"), None)
    return jax.shard_map(
        per_device, mesh=mesh, in_specs=(spec,) * 6, out_specs=(spec,) * 3, check_vma=False
    )
```

```python
import math

import jax
import jax.numpy as jnp
from jax import lax
from jax.experimental import pallas as pl
from jax.experimental.pallas import tpu as pltpu
from jax.sharding import PartitionSpec as P

MESH = pl.DeviceIdType.MESH
HD = 128
SCALE = HD**-0.5
LOG2E = math.log2(math.e)
F32 = jnp.float32
BF16 = jnp.bfloat16
NX = 4
SLOTS = 2 * NX
BLOCKS = 4
ROWS = SLOTS * 128
HALF = 256


def nt(a, b, **kw):
    return lax.dot_general(a, b, (((1,), (1,)), ((), ())), preferred_element_type=F32, **kw)


def nn(a, b, **kw):
    return lax.dot_general(a, b, (((1,), (0,)), ((), ())), preferred_element_type=F32, **kw)


def tn(a, b):
    return lax.dot_general(a, b, (((0,), (0,)), ((), ())), preferred_element_type=F32)


def tile(k, v, q, g, lse, delta):
    p = jnp.exp2(nt(k, q) * (SCALE * LOG2E) - lse)
    ds = (p * (nt(v, g) - delta)).astype(BF16)
    dv = nn(p.astype(BF16), g)
    dk = nn(ds, q)
    dq = tn(ds, k)
    return dk, dv, dq


def kernel(
    groups,
    q_in, k_in, v_in, o_in, g_in, l_in,
    dq_res, dk_res, dv_res,
    qg, kv, kvp, eqg, st_all, st, est, g_v, o_v, l_v,
    dq_edge, dq_own, dk_acc, dv_acc,
    dq_oth, dq_got, dq_out, dk_out, dv_out, dqe_out, dqe_got, dkv_out, dkv_got,
    loc, r_qg, r_kv, r_b, r_k, r_c, r_st, r_dqe, r_dkv, r_d, r_out,
    s_a, s_b, s_k, s_c, s_st, s_st2, s_dqe, s_dkv, s_d, s_out, s_dl, r_dl,
):
    head = lax.axis_index("head")
    blk = lax.axis_index("blk")
    x = lax.div(head, 2)
    zl = lax.rem(head, 2)
    grp = lax.div(blk, 2)
    c = lax.rem(blk, 2)
    me_t = x * 2 + c
    me_s = c * NX + x
    eb = 3 * zl
    pb = 3 - eb
    partner = (x * 2 + (1 - zl), blk)
    near = (x * 2 + (1 - zl), lax.rem(grp + 2 * zl - 1 + groups, groups) * 2 + c)
    order = [pb + i * (2 * zl - 1) for i in range(BLOCKS)]
    twin = [(x, 1 - c)]
    others = [(lax.rem(x + dx, NX), cc) for dx in (1, 3, 2) for cc in range(2)]

    def device_at(xt, ct):
        return (xt * 2 + zl, grp * 2 + ct)

    def rows(b):
        return pl.ds(pl.multiple_of(b * HALF, HALF), HALF)

    def run(s):
        return pl.ds(pl.multiple_of(s * 128, 128), 128)

    def cols(t, hl):
        return pl.ds(pl.multiple_of(t * 256 + hl * 128, 128), 128)

    def remote(src, dst, ssem, rsem, device):
        copy = pltpu.make_async_remote_copy(
            src_ref=src, dst_ref=dst, send_sem=ssem, recv_sem=rsem, device_id=device, device_id_type=MESH
        )
        copy.start()
        return copy

    def arrived(ref, sem):
        pltpu.make_async_copy(ref, ref, sem).wait()

    pending = []

    def arrays(hl, which):
        if which == 0:
            sem = r_qg.at[hl, me_s]
            return ((q_in, qg.at[0, 0, hl], 0, sem), (g_in, qg.at[0, 1, hl], 1, sem))
        sem = r_kv.at[hl]
        return ((k_in, kv.at[0, hl], 2, sem), (v_in, kv.at[1, hl], 3, sem))

    for hl in range(2):
        for src, dst, _, sem in arrays(hl, 0):
            pltpu.make_async_copy(src.at[:, cols(me_t, hl)], dst.at[run(me_s)], sem).start()
    locals_ = [
        pltpu.make_async_copy(g_in, g_v, loc.at[0]),
        pltpu.make_async_copy(o_in, o_v, loc.at[1]),
        pltpu.make_async_copy(l_in, l_v, loc.at[2]),
    ]
    for copy in locals_:
        copy.start()
    for hl in range(2):
        for src, dst, _, sem in arrays(hl, 1):
            pltpu.make_async_copy(src.at[:, cols(me_t, hl)], dst.at[run(me_s)], sem).start()

    barrier = pltpu.get_barrier_semaphore()
    for device in [device_at(*t) for t in twin + others] + [partner, near]:
        pl.semaphore_signal(barrier, inc=1, device_id=device, device_id_type=MESH)
    pl.semaphore_wait(barrier, SLOTS + 1)

    def spread(hl, which, targets):
        for xt, ct in targets:
            for src, dst, n, sem in arrays(hl, which):
                remote(
                    src.at[:, cols(xt * 2 + ct, hl)], dst.at[run(me_s)], s_a.at[n, hl], sem, device_at(xt, ct)
                )

    def forward(hl, s):
        arrived(qg.at[0, :, hl, run(s)], r_qg.at[hl, s])
        pending.append(remote(
            qg.at[0, :, hl, run(s)], qg.at[1, :, hl, run(s)], s_b.at[hl, s], r_b.at[hl, lax.div(s, 2)], partner
        ))

    forward(0, me_s)
    spread(0, 0, twin)
    spread(0, 0, others)
    spread(1, 0, twin)
    forward(1, me_s)
    twin_s = (1 - c) * NX + x
    for hl in range(2):
        forward(hl, twin_s)

    for copy in locals_:
        copy.wait()
    col = lax.broadcasted_iota(jnp.int32, (SLOTS * 256, 128), 0)
    r = lax.broadcasted_iota(jnp.int32, (SLOTS * 256, 128), 1)
    wanted = lax.shift_right_logical(r, 3) * 2 + lax.shift_right_logical(r & 7, 1)
    pick = jnp.where(
        (lax.shift_right_logical(col, 7) == wanted) & ((r & 1) == 1) & ((r & 7) < 4), 1.0, 0.0
    ).astype(BF16)
    prod = g_v[...].astype(F32) * o_v[...].astype(F32)
    high = prod.astype(BF16)
    low = (prod - high.astype(F32)).astype(BF16)
    sums = nn(high, pick) + nn(low, pick)
    st_all[...] = jnp.transpose(sums)[: 8 * SLOTS]
    for h in range(2 * SLOTS):
        place = 8 * (h // 2) + 2 * (h % 2)
        st_all[place : place + 1, :] = l_v[h : h + 1, :] * LOG2E
    mine = st_all.at[pl.ds(pl.multiple_of(me_t * 8, 8), 8)]
    pltpu.make_async_copy(mine, st.at[0, me_s], r_st.at[0]).start()
    for n, (xt, ct) in enumerate(twin + others):
        pending.append(remote(
            st_all.at[pl.ds(pl.multiple_of((xt * 2 + ct) * 8, 8), 8)],
            st.at[0, me_s], s_st.at[n], r_st.at[0], device_at(xt, ct),
        ))

    spread(0, 1, twin + others)

    rest = [cc * NX + lax.rem(x + dx, NX) for dx in (3, 1, 2) for cc in range(2)]
    for s in rest[:4]:
        forward(0, s)
    spread(1, 0, others)
    arrived(st.at[0], r_st.at[0])
    pending.append(remote(st.at[0], st.at[1], s_st2.at[0], r_st.at[1], partner))
    for s in rest[4:]:
        forward(0, s)
    spread(1, 1, twin + others)

    dk_acc[...] = jnp.zeros_like(dk_acc)
    dv_acc[...] = jnp.zeros_like(dv_acc)

    def forward_kv(hl):
        arrived(kv.at[:, hl], r_kv.at[hl])
        pending.append(remote(kv.at[:, hl, rows(pb)], kvp.at[hl], s_k.at[hl], r_k.at[hl], partner))

    def forward_own_edge(hl):
        pending.append(remote(
            qg.at[0, :, hl, rows(eb)], eqg.at[hl, :, pl.ds(0, HALF)], s_c.at[hl, 0], r_c.at[hl], near
        ))

    def forward_edge(hl):
        arrived(qg.at[1, :, hl, rows(eb)], r_b.at[hl, eb])
        pending.append(remote(
            qg.at[1, :, hl, rows(eb)], eqg.at[hl, :, pl.ds(HALF, HALF)], s_c.at[hl, 1], r_c.at[hl], near
        ))

    def stat(ref, parities, first, hl, n):
        place = 2 * hl + n
        return jnp.concatenate(
            [ref[p, first + j, place : place + 1, :] for p in parities for j in range(2)], axis=1
        )

    def queries(hl, parity, i):
        b = order[i]
        if parity == 1 and i < BLOCKS - 1:
            arrived(qg.at[1, :, hl, rows(b)], r_b.at[hl, b])
        count = (2 if i in (0, BLOCKS - 1) else 3) * HALF
        keys = pl.ds(pl.multiple_of(jnp.maximum(b - 1, 0) * HALF, HALF), count)
        dk, dv, dq = tile(
            kv[0, hl, keys], kv[1, hl, keys], qg[parity, 0, hl, rows(b)], qg[parity, 1, hl, rows(b)],
            stat(st, (parity,), 2 * b, hl, 0), stat(st, (parity,), 2 * b, hl, 1),
        )
        dk_acc[hl, keys] += dk
        dv_acc[hl, keys] += dv
        dq = dq * SCALE
        if parity == 0:
            dq_own[hl, rows(b)] = dq
        elif i == BLOCKS - 1:
            dq_edge[hl] = dq
        else:
            dq_oth[hl, rows(b)] = dq.astype(BF16)

    def edge(hl):
        arrived(kvp.at[hl], r_k.at[hl])
        arrived(eqg.at[hl], r_c.at[hl])
        dk, dv, dq = tile(
            jnp.concatenate([kvp[hl, 0], kv[0, hl, rows(eb)]], axis=0),
            jnp.concatenate([kvp[hl, 1], kv[1, hl, rows(eb)]], axis=0),
            eqg[hl, 0], eqg[hl, 1], stat(est, (0, 1), 0, hl, 0), stat(est, (0, 1), 0, hl, 1),
        )
        dqe_out[hl] = (dq * SCALE).astype(BF16)
        pending.append(remote(dqe_out.at[hl], dqe_got.at[hl], s_dqe.at[hl], r_dqe.at[hl], near))
        dkv_out[hl, 0] = (dk[:HALF] * SCALE).astype(BF16)
        dkv_out[hl, 1] = dv[:HALF].astype(BF16)
        dk_acc[hl, rows(eb)] += dk[HALF:]
        dv_acc[hl, rows(eb)] += dv[HALF:]

    def send_edge_keys(hl):
        pending.append(remote(dkv_out.at[hl], dkv_got.at[hl], s_dkv.at[hl], r_dkv.at[hl], partner))

    def send_queries(hl, i):
        b = order[i]
        if i == BLOCKS - 1:
            arrived(dqe_got.at[hl], r_dqe.at[hl])
            dq_oth[hl, rows(b)] = (dq_edge[hl] + dqe_got[hl, pl.ds(HALF, HALF)].astype(F32)).astype(BF16)
        if hl == 1 and i == BLOCKS - 1:
            for j in range(2):
                pending.append(remote(
                    dq_oth.at[hl, run(2 * b + j)], dq_got.at[hl, run(2 * b + j)], s_dl.at[j], r_dl.at[j], partner
                ))
        else:
            pending.append(remote(
                dq_oth.at[hl, rows(b)], dq_got.at[hl, rows(b)], s_d.at[hl, b], r_d.at[hl, b], partner
            ))

    def give_back(buf, res, n, hl, b, runs=(0, 1)):
        for j in runs:
            s = 2 * b + j
            src = buf.at[hl, run(s)]
            dst = res.at[:, cols(me_t, hl)]

            @pl.when(s == me_s)
            def _():
                pltpu.make_async_copy(src, dst, r_out.at[n]).start()

            @pl.when(s != me_s)
            def _():
                remote(src, dst, s_out.at[n], r_out.at[n], device_at(lax.rem(s, NX), lax.div(s, NX)))

    def finish_keys(hl, i):
        b = order[i]
        dk = dk_acc[hl, rows(b)] * SCALE
        dv = dv_acc[hl, rows(b)]
        if i == 0:
            arrived(dkv_got.at[hl], r_dkv.at[hl])
            dk = dk + dkv_got[hl, 0].astype(F32)
            dv = dv + dkv_got[hl, 1].astype(F32)
        dk_out[hl, rows(b)] = dk.astype(BF16)
        dv_out[hl, rows(b)] = dv.astype(BF16)
        give_back(dk_out, dk_res, 1, hl, b)
        give_back(dv_out, dv_res, 2, hl, b)

    def finish_last():
        for j in range(2):
            s = 2 * order[0] + j
            arrived(dq_got.at[1, run(s)], r_dl.at[j])
            dq_out[1, run(s)] = (dq_own[1, run(s)] + dq_got[1, run(s)].astype(F32)).astype(BF16)
            give_back(dq_out, dq_res, 0, 1, order[0], (j,))

    def finish_queries(hl, i):
        b = order[i]
        arrived(dq_got.at[hl, rows(b)], r_d.at[hl, b])
        dq = dq_own[hl, rows(b)] + dq_got[hl, rows(b)].astype(F32)
        if i == BLOCKS - 1:
            dq = dq + dqe_got[hl, pl.ds(0, HALF)].astype(F32)
        dq_out[hl, rows(b)] = dq.astype(BF16)
        give_back(dq_out, dq_res, 0, hl, b)

    forward_own_edge(0)
    forward_kv(0)
    for i in range(BLOCKS):
        queries(0, 0, i)
    for s in rest[:4]:
        forward(1, s)
    forward_edge(0)
    arrived(st.at[1], r_st.at[1])
    pending.append(remote(st.at[:, pl.ds(2 * eb, 2)], est, s_st2.at[1], r_st.at[2], near))
    for i in (3, 2):
        queries(0, 1, i)
    for s in rest[4:]:
        forward(1, s)
    forward_own_edge(1)
    for i in (1, 0):
        queries(0, 1, i)
    arrived(est, r_st.at[2])
    edge(0)
    for i in (2, 1, 3):
        finish_keys(0, i)
    send_queries(0, 2)
    forward_edge(1)
    forward_kv(1)
    for i in (1, 0):
        send_queries(0, i)
    send_edge_keys(0)
    for i in range(BLOCKS):
        queries(1, 0, i)
    send_queries(0, 3)
    for i in (3, 2, 1, 0):
        queries(1, 1, i)
    for i in (2, 1):
        finish_keys(1, i)
    edge(1)
    send_edge_keys(1)
    for i in (2, 1, 0):
        send_queries(1, i)
    finish_keys(1, 3)
    for i in (1, 2, 3):
        finish_queries(0, i)
    finish_keys(0, 0)
    send_queries(1, 3)
    finish_queries(0, 0)
    finish_keys(1, 0)
    for i in (1, 2, 3):
        finish_queries(1, i)
    finish_last()

    for copy in pending:
        copy.wait_send()
    for n in range(4):
        for hl in range(2):
            arrived(kv.at[0, 0, pl.ds(0, 7 * 128)], s_a.at[n, hl])
    for n, res in enumerate((dq_res, dk_res, dv_res)):
        arrived(dk_out.at[:, pl.ds(0, 7 * 128)], s_out.at[n])
        arrived(res, r_out.at[n])


def copy_kernel(a_ref, b_ref, c_ref, a_res, b_res, c_res, held, sems):
    refs = ((a_ref, a_res), (b_ref, b_res), (c_ref, c_res))
    loads = [pltpu.make_async_copy(src, held.at[n], sems.at[0, n]) for n, (src, _) in enumerate(refs)]
    stores = [pltpu.make_async_copy(held.at[n], dst, sems.at[1, n]) for n, (_, dst) in enumerate(refs)]
    for load in loads:
        load.start()
    for load, store in zip(loads, stores):
        load.wait()
        store.start()
    for store in stores:
        store.wait()


def per_device(queries, keys, values, outputs, out_grad, log_sum):
    groups = lax.axis_size("blk") // 2
    tokens, width = queries.shape
    any_ = pl.BlockSpec(memory_space=pl.ANY)
    dma = pltpu.SemaphoreType.DMA
    result = jax.ShapeDtypeStruct((tokens, width), BF16)
    scratch = [
        pltpu.VMEM((2, 2, 2, ROWS, HD), BF16),
        pltpu.VMEM((2, 2, ROWS, HD), BF16),
        pltpu.VMEM((2, 2, HALF, HD), BF16),
        pltpu.VMEM((2, 2, 2 * HALF, HD), BF16),
        pltpu.VMEM((8 * SLOTS, 128), F32),
        pltpu.VMEM((2, SLOTS, 8, 128), F32),
        pltpu.VMEM((2, 2, 8, 128), F32),
        pltpu.VMEM((tokens, width), BF16),
        pltpu.VMEM((tokens, width), BF16),
        pltpu.VMEM(log_sum.shape[::-1], F32),
        pltpu.VMEM((2, HALF, HD), F32),
        pltpu.VMEM((2, ROWS, HD), F32),
        pltpu.VMEM((2, ROWS, HD), F32),
        pltpu.VMEM((2, ROWS, HD), F32),
        pltpu.VMEM((2, ROWS, HD), BF16),
        pltpu.VMEM((2, ROWS, HD), BF16),
        pltpu.VMEM((2, ROWS, HD), BF16),
        pltpu.VMEM((2, ROWS, HD), BF16),
        pltpu.VMEM((2, ROWS, HD), BF16),
        pltpu.VMEM((2, 2 * HALF, HD), BF16),
        pltpu.VMEM((2, 2 * HALF, HD), BF16),
        pltpu.VMEM((2, 2, HALF, HD), BF16),
        pltpu.VMEM((2, 2, HALF, HD), BF16),
        dma((3,)),
        dma((2, SLOTS)),
        dma((2,)),
        dma((2, BLOCKS)),
        dma((2,)),
        dma((2,)),
        dma((3,)),
        dma((2,)),
        dma((2,)),
        dma((2, BLOCKS)),
        dma((3,)),
        dma((4, 2)),
        dma((2, SLOTS)),
        dma((2,)),
        dma((2, 2)),
        dma((SLOTS,)),
        dma((2,)),
        dma((2,)),
        dma((2,)),
        dma((2, BLOCKS)),
        dma((3,)),
        dma((2,)),
        dma((2,)),
    ]

    def body(*refs):
        kernel(groups, *refs)

    grads = pl.pallas_call(
        body,
        out_shape=(result, result, result),
        in_specs=[any_] * 6,
        out_specs=(any_, any_, any_),
        scratch_shapes=scratch,
        compiler_params=pltpu.CompilerParams(
            collective_id=0, has_side_effects=True, vmem_limit_bytes=60 * 2**20
        ),
        cost_estimate=pl.CostEstimate(flops=4 * 10**9, bytes_accessed=4 * 2**20, transcendentals=3 * 2**20),
        name="attention_backward",
    )(queries, keys, values, outputs, out_grad, jnp.transpose(log_sum))
    return pl.pallas_call(
        copy_kernel,
        out_shape=(result, result, result),
        in_specs=[any_] * 3,
        out_specs=(any_, any_, any_),
        scratch_shapes=[pltpu.VMEM((3, tokens, width), BF16), dma((2, 3))],
        compiler_params=pltpu.CompilerParams(vmem_limit_bytes=60 * 2**20),
        name="results",
    )(*grads)


def solution(mesh):
    spec = P(("blk", "head"), None)
    return jax.shard_map(
        per_device, mesh=mesh, in_specs=(spec,) * 6, out_specs=(spec,) * 3, check_vma=False
    )
```
